512 devices in a mesh: areal: 32 (over y, x, core), layer: 16 (over z).
Axes of the slice: x: 4, y: 4, z: 16, core: 2. Of those that a mesh axis runs over, the one named last changes fastest.
Arguments:
- rhs: bfloat16 [32, 32, 112, 384], P('areal', 'layer'), may hold values from -6 to 6
- areal_blocks: bfloat16 [32, 32, 6, 384, 384], P('areal', 'layer'), may hold values from -0.078125 to 0.078125
- vertical_blocks: bfloat16 [32, 32, 2, 384, 384], P('areal', 'layer'), may hold values from -0.078125 to 0.078125
- conn_src: int32 [32, 16, 6], P('areal', 'layer'), may hold values from 0 to 63, as said below
- conn_count: int32 [32, 16], P('areal', 'layer'), may hold values from 1 to 6, as said below
- tile_map: int32 [64], replicated, may hold values from 0 to 63, as said below
- well_cells: int32 [32, 32, 4], P('areal', 'layer'), may hold values from 0 to 127
- well_gain: float32 [32, 32, 4], P('areal', 'layer'), may hold values from -24 to 24
- sens: float32 [32, 32, 3, 128], P('areal', 'layer'), may hold values from -6 to 6
- basis: bfloat16 [32, 32, 128, 256], P('areal', 'layer'), may hold values from -0.015625 to 0.015625
Outputs:
- adjoint: bfloat16 [32, 32, 112, 384], P('areal', 'layer')
- coefficients: bfloat16 [112, 256], P('layer', 'areal')
The draws below stay inside these ranges and needn't reach their ends.
Inputs may be any that keep to these rules, and one draw needn't show every extreme that they name: Tile t of a layer group's plane is held by device column tile_map[t] // 2 in tile layer 2 g + tile_map[t] % 2; each value is held by one tile. `conn_src`: the 6 sources of device column c lie, in some order, on the 6 device columns (c + k) mod 32 with k one of 1 to 2, their negatives, 16 and 17, one on each. `conn_count`: the live connections of a device are its first ones. `well_cells`: cells of a tile, repeats allowed.
All inputs are finite; a program needn't handle non-finite values.
Results may differ from the reference program's by a relative error of at most 0.02.
Values may be sent and summed in bfloat16 or wider, within the bound.
A program may use at most 64 MiB of HBM per device.

```python
import jax
import jax.numpy as jnp
from jax import lax

CELLS = 128
PHASES = 3
UNKNOWNS = 384
MODES = 256
RHS = 112
NS = 6
WELLS = 4
ITERS = 3
COLUMNS = 32
GROUPS = 16
LAYERS = 32


def common_map(key):
    return jax.random.permutation(jax.random.fold_in(key, 7), 2 * COLUMNS).astype(jnp.int32)


def draw_tile_map(key, part):
    return common_map(key)


def draw_conn_src(key, part):
    placed = common_map(key)
    holder = jnp.argsort(placed, stable=True).astype(jnp.int32)
    half = NS // 2 - 1
    reach = jnp.arange(1, half + 1, dtype=jnp.int32)
    far_reach = jnp.array([COLUMNS // 2, COLUMNS // 2 + 1], dtype=jnp.int32)
    deltas = jnp.concatenate([reach, -reach, far_reach]).astype(jnp.int32)
    keys = jax.random.split(jax.random.fold_in(key, 13), COLUMNS * GROUPS)
    order = jax.vmap(lambda one: jax.random.permutation(one, NS))(keys)
    offsets = deltas[order.reshape(COLUMNS, GROUPS, NS).astype(jnp.int32)]
    column = jnp.arange(COLUMNS, dtype=jnp.int32)[:, None, None]
    peer = (column + offsets + COLUMNS) % COLUMNS
    slot = jax.random.randint(jax.random.fold_in(key, 17), (COLUMNS, GROUPS, NS), 0, 2).astype(jnp.int32)
    return holder[peer * 2 + slot].astype(jnp.int32)


def draw_conn_count(key, part):
    total = COLUMNS * GROUPS
    counts = jax.random.randint(jax.random.fold_in(key, 19), (total,), 1, NS + 1).astype(jnp.int32)
    first = jax.random.randint(jax.random.fold_in(key, 23), (), 0, total).astype(jnp.int32)
    second = (first + 1 + jax.random.randint(jax.random.fold_in(key, 29), (), 0, total - 1).astype(jnp.int32)) % total
    spots = jnp.arange(total, dtype=jnp.int32)
    counts = jnp.where(spots == first, NS, jnp.where(spots == second, 1, counts))
    return counts.reshape(COLUMNS, GROUPS).astype(jnp.int32)


def touch_ends(values, key, least, largest):
    spot = [jax.random.randint(jax.random.fold_in(key, axis), (), 0, length) for axis, length in enumerate(values.shape)]
    widest = values.shape.index(max(values.shape))
    next_to = spot[:widest] + [(spot[widest] + 1) % values.shape[widest]] + spot[widest + 1:]
    return values.at[tuple(spot)].set(least).at[tuple(next_to)].set(largest)


def steps_of(own_key, dims, cuts, low, high):
    def one(axis_at, blocks):
        steps = jax.random.uniform(jax.random.fold_in(jax.random.fold_in(own_key, 6), axis_at), (blocks,), jnp.float32, low / len(cuts), high / len(cuts))
        return jnp.repeat(jnp.exp(steps), dims[axis_at] // blocks).reshape((-1,) + (1,) * (len(dims) - axis_at - 1))

    loudness = one(*cuts[0])
    for cut in cuts[1:]:
        loudness = loudness * one(*cut)
    return loudness


def gaussian(own_key, shape, deviation, bound, cuts=(), held_as=jnp.bfloat16):
    values = deviation * jax.random.normal(own_key, shape, jnp.float32)
    if cuts:
        values = values * steps_of(own_key, shape, cuts, -0.22, 0.18)
    return jnp.clip(values, -bound, bound).astype(held_as)


def setup_inputs(seed: int = 0) -> dict:
    splits = jax.random.split(jax.random.key(seed), 11)
    rhs = gaussian(splits[0], (COLUMNS, LAYERS, RHS, UNKNOWNS), 1.0, 6.0, ((0, 32), (1, 16)))
    areal_blocks = gaussian(splits[1], (COLUMNS, LAYERS, NS, UNKNOWNS, UNKNOWNS), (2 * UNKNOWNS * (NS + 2)) ** -0.5, 0.078125, ((0, 32), (1, 16)))
    vertical_blocks = gaussian(splits[2], (COLUMNS, LAYERS, 2, UNKNOWNS, UNKNOWNS), (2 * UNKNOWNS * (NS + 2)) ** -0.5, 0.078125, ((0, 32), (1, 16)))
    conn_src = draw_conn_src(jax.random.fold_in(splits[10], 71), 0)
    conn_count = draw_conn_count(jax.random.fold_in(splits[10], 71), 0)
    tile_map = draw_tile_map(jax.random.fold_in(splits[10], 71), 0)
    well_cells = touch_ends(jax.random.randint(splits[6], (COLUMNS, LAYERS, WELLS), 0, CELLS), jax.random.fold_in(splits[6], 1), 0, CELLS - 1).astype(jnp.int32)
    well_gain = gaussian(splits[7], (COLUMNS, LAYERS, WELLS), 4.0, 24.0, ((0, 32), (1, 16)), jnp.float32)
    sens = gaussian(splits[8], (COLUMNS, LAYERS, PHASES, CELLS), 1.0, 6.0, ((0, 32), (1, 16)), jnp.float32)
    basis = gaussian(splits[9], (COLUMNS, LAYERS, CELLS, MODES), (CELLS * LAYERS * COLUMNS) ** -0.5, 0.015625, ((0, 32), (1, 16)))
    return dict(rhs=rhs, areal_blocks=areal_blocks, vertical_blocks=vertical_blocks, conn_src=conn_src, conn_count=conn_count, tile_map=tile_map, well_cells=well_cells, well_gain=well_gain, sens=sens, basis=basis)


def apply_once(lam, rhs, areal_blocks, vertical_blocks, peer, slot, live):
    zero = jnp.zeros_like(lam[:, :1])
    below = jnp.concatenate([zero, lam[:, :-1]], axis=1)
    above = jnp.concatenate([lam[:, 1:], zero], axis=1)
    layer_pos = 2 * jnp.arange(GROUPS, dtype=jnp.int32)

    def per_column(column):
        peer_col = peer[column]
        slot_col = slot[column]
        chosen = lam[peer_col, layer_pos[:, None] + slot_col]
        chosen = jnp.where(live[column][:, :, None, None], chosen, jnp.zeros_like(chosen))
        blocks = areal_blocks[column].reshape(GROUPS, 2, NS, UNKNOWNS, UNKNOWNS)
        areal = jnp.einsum("gsru,gdsuv->gdrv", chosen.astype(jnp.float32), blocks.astype(jnp.float32))
        areal = areal.reshape(LAYERS, RHS, UNKNOWNS)
        vblocks = vertical_blocks[column].astype(jnp.float32)
        vert = jnp.einsum("jru,juv->jrv", below[column].astype(jnp.float32), vblocks[:, 0])
        vert = vert + jnp.einsum("jru,juv->jrv", above[column].astype(jnp.float32), vblocks[:, 1])
        return areal + vert

    off = lax.map(per_column, jnp.arange(COLUMNS, dtype=jnp.int32))
    return (rhs.astype(jnp.float32) - off).astype(jnp.bfloat16)


def reference(rhs, areal_blocks, vertical_blocks, conn_src, conn_count, tile_map, well_cells, well_gain, sens, basis):
    place = tile_map[conn_src]
    peer = place // 2
    slot = place % 2
    live = jnp.arange(NS, dtype=jnp.int32)[None, None, :] < conn_count[:, :, None]
    lam = rhs
    for step in range(ITERS):
        lam = apply_once(lam, rhs, areal_blocks, vertical_blocks, peer, slot, live)
    lamf = lam.astype(jnp.float32).reshape(COLUMNS, LAYERS, RHS, PHASES, CELLS)
    grad = jnp.sum(lamf * sens[:, :, None, :, :], axis=3)
    hits = well_cells[:, :, :, None] == jnp.arange(CELLS, dtype=jnp.int32)[None, None, None, :]
    well_sum = jnp.sum(jnp.where(hits, well_gain[:, :, :, None], 0.0), axis=2)
    grad = (grad + well_sum[:, :, None, :] * lamf[:, :, :, 0, :]).astype(jnp.bfloat16)
    coefficients = jnp.einsum("ajrc,ajcm->rm", grad.astype(jnp.float32), basis.astype(jnp.float32))
    return lam, coefficients.astype(jnp.bfloat16)
```

```python
import jax
import jax.numpy as jnp
from jax import lax
from jax.experimental import pallas as pl
from jax.experimental.pallas import tpu as pltpu
from jax.sharding import PartitionSpec as P

ITERS = 3
COLUMNS = 32
GROUPS = 16
ROWS = 112
U = 384
CELLS = 128
MODES = 256
NS = 6
WELLS = 4
PER = ROWS // GROUPS
OFFSETS = (1, 2, -1, -2, 16, 17)
ORDER = (5, 4, 0, 1, 2, 3)
CHUNKS = ((0, 64), (64, 48))
MESH = pl.DeviceIdType.MESH
F32, BF16, I32 = jnp.float32, jnp.bfloat16, jnp.int32


def kernel(
    conn_src,
    conn_count,
    tile_map,
    well_cells,
    well_gain,
    rhs_hbm,
    areal_hbm,
    vert_hbm,
    sens_hbm,
    basis_hbm,
    adjoint_hbm,
    coef_ref,
    lam,
    w,
    v,
    sens,
    basis,
    send,
    recvz,
    req_out,
    req_in,
    part,
    part_in,
    scat,
    scat_in,
    adj,
    *rest,
):
    recv = [[rest[i * len(CHUNKS) + h] for h in range(len(CHUNKS))] for i in range(ITERS)]
    (
        load_sem,
        out_sem,
        req_ss,
        req_rs,
        a_ss,
        a_rs,
        z_ss,
        z_rs,
        p_ss,
        p_rs,
        s_ss,
        s_rs,
    ) = rest[ITERS * len(CHUNKS) :]
    c, g = lax.axis_index("areal"), lax.axis_index("layer")

    loads = [
        pltpu.make_async_copy(rhs_hbm.at[0], lam.at[0, pl.ds(0, 2)], load_sem.at[0]),
        pltpu.make_async_copy(vert_hbm.at[0], v, load_sem.at[1]),
        pltpu.make_async_copy(areal_hbm.at[0], w, load_sem.at[2]),
        pltpu.make_async_copy(sens_hbm.at[0], sens, load_sem.at[3]),
        pltpu.make_async_copy(basis_hbm.at[0], basis, load_sem.at[4]),
    ]
    for one in loads:
        one.start()

    barrier = pltpu.get_barrier_semaphore()
    for k in range(1, COLUMNS):
        pl.semaphore_signal(barrier, inc=1, device_id=(lax.rem(c + k, COLUMNS), g), device_id_type=MESH)
    for k in range(1, GROUPS):
        pl.semaphore_signal(barrier, inc=1, device_id=(c, lax.rem(g + k, GROUPS)), device_id_type=MESH)

    count = conn_count[0, 0]
    where, wanted = [], []
    for s in range(NS):
        place = tile_map[conn_src[0, 0, s]]
        delta = lax.rem((place >> 1) - c + COLUMNS, COLUMNS)
        at = I32(0)
        for k, offset in enumerate(OFFSETS):
            at = jnp.where(delta == offset % COLUMNS, I32(k), at)
        where.append(at)
        wanted.append(jnp.where(s < count, place & 1, I32(2)))
    for k in range(NS):
        ask = I32(2)
        for s in range(NS):
            ask = jnp.where(where[s] == k, wanted[s], ask)
        req_out[k] = jnp.full((8, 128), ask, I32)
    part[...] = jnp.zeros((COLUMNS, 8, 128), F32)
    for i in range(ITERS):
        lam[i, 2] = jnp.zeros((ROWS, U), BF16)

    pl.semaphore_wait(barrier, COLUMNS + GROUPS - 2)

    asks = []
    for k in ORDER:
        one = pltpu.make_async_remote_copy(
            req_out.at[k], req_in.at[k], req_ss.at[k], req_rs.at[k],
            device_id=(lax.rem(c + OFFSETS[k] + COLUMNS, COLUMNS), g), device_id_type=MESH,
        )
        one.start()
        asks.append(one)

    up, down = lax.rem(g + 1, GROUPS), lax.rem(g + GROUPS - 1, GROUPS)

    def send_vertical(i, h):
        first, rows = CHUNKS[h]
        at = pl.ds(first, rows)
        out = []
        for side, to in ((0, up), (1, down)):
            one = pltpu.make_async_remote_copy(
                lam.at[i, 1 - side, at], recvz.at[i, side, at], z_ss.at[i, h, side], z_rs.at[i, h, side],
                device_id=(c, to), device_id_type=MESH,
            )
            one.start()
            out.append(one)
        return out

    def send_areal(i, h, slots):
        first, rows = CHUNKS[h]
        at = pl.ds(first, rows)
        out = []
        for k in ORDER:
            send[i, k, at] = lam[i, slots[k], at]
            one = pltpu.make_async_remote_copy(
                send.at[i, k, at], recv[i][h].at[k], a_ss.at[i, h, k], a_rs.at[i, h, k],
                device_id=(lax.rem(c - OFFSETS[k] + COLUMNS, COLUMNS), g), device_id_type=MESH,
            )
            one.start()
            out.append(one)
        return out

    flying = {}
    loads[0].wait()
    for h in range(len(CHUNKS)):
        flying[0, h] = send_vertical(0, h)
    for one in asks:
        one.wait_recv()
    slots = [jnp.max(req_in[k]) for k in range(NS)]
    for h in range(len(CHUNKS)):
        flying[0, h] = flying[0, h] + send_areal(0, h, slots)

    for one in loads[1:]:
        one.wait()

    cell = lax.broadcasted_iota(I32, (1, CELLS), 1)
    weight = []
    for d in range(2):
        wells = jnp.zeros((1, CELLS), F32)
        for k in range(WELLS):
            wells += jnp.where(cell == well_cells[0, d, k], well_gain[0, d, k], 0.0)
        weight.append([sens[d, 0:1] + wells, sens[d, 1:2], sens[d, 2:3]])

    stored = []
    for i in range(ITERS):
        for h, (first, rows) in enumerate(CHUNKS):
            at = pl.ds(first, rows)
            for one in flying[i, h]:
                one.wait_recv()
            below = jnp.where(g > 0, recvz[i, 0, at], jnp.zeros((rows, U), BF16))
            above = jnp.where(g < GROUPS - 1, recvz[i, 1, at], jnp.zeros((rows, U), BF16))
            sides = ((below, lam[i, 1, at]), (lam[i, 0, at], above))
            chosen = jnp.concatenate([recv[i][h][where[s]] for s in range(NS)], axis=1)
            grads = []
            for d in range(2):
                off = jnp.dot(chosen, w[d].reshape(NS * U, U), preferred_element_type=F32)
                near = jnp.concatenate(sides[d], axis=1)
                off += jnp.dot(near, v[d].reshape(2 * U, U), preferred_element_type=F32)
                new = (lam[0, d, at].astype(F32) - off).astype(BF16)
                if i < ITERS - 1:
                    lam[i + 1, d, at] = new
                else:
                    adj[d, at] = new
                    newf = new.astype(F32)
                    grad = newf[:, :CELLS] * weight[d][0]
                    for p in range(1, 3):
                        grad += newf[:, p * CELLS : (p + 1) * CELLS] * weight[d][p]
                    grads.append(grad.astype(BF16))
            if i < ITERS - 1:
                flying[i + 1, h] = send_areal(i + 1, h, slots) + send_vertical(i + 1, h)
            else:
                grad = jnp.concatenate(grads, axis=1)
                scat_rows = jnp.dot(grad, basis[...].reshape(2 * CELLS, MODES), preferred_element_type=F32)
                part[:, :, first : first + rows] = scat_rows.T.reshape(COLUMNS, 8, rows)

    store = pltpu.make_async_copy(adj, adjoint_hbm.at[0], out_sem)
    store.start()

    parts = []
    for k in range(1, COLUMNS):
        to = lax.rem(c + k, COLUMNS)
        one = pltpu.make_async_remote_copy(
            part.at[to], part_in.at[k], p_ss.at[k], p_rs.at[k], device_id=(to, g), device_id_type=MESH
        )
        one.start()
        parts.append(one)

    big = lax.broadcasted_iota(I32, (8 * 128, 128), 0)
    lane = lax.broadcasted_iota(I32, (8 * 128, 128), 1)
    row = big & 127
    pick = jnp.where((row < ROWS) & (lane == 8 * lax.rem(row, PER) + (big >> 7)), 1.0, 0.0).astype(BF16)
    group = lax.broadcasted_iota(I32, (GROUPS, 128), 0)
    held = lax.broadcasted_iota(I32, (GROUPS, 128), 1)
    mine = (held >= PER * group) & (held < PER * group + PER)

    total = part[c]
    for one in parts:
        one.wait_recv()
    for k in range(1, COLUMNS):
        total += part_in[k]
    spread = jnp.concatenate(
        [jnp.where(mine, jnp.broadcast_to(total[m : m + 1], (GROUPS, 128)), 0.0).astype(BF16) for m in range(8)],
        axis=1,
    )
    packed = jnp.dot(spread, pick, preferred_element_type=F32)
    scat[...] = packed.reshape(GROUPS, 1, 128)

    scats = []
    for k in range(1, GROUPS):
        to = lax.rem(g + k, GROUPS)
        one = pltpu.make_async_remote_copy(
            scat.at[to], scat_in.at[k], s_ss.at[k], s_rs.at[k], device_id=(c, to), device_id_type=MESH
        )
        one.start()
        scats.append(one)
    line = scat[g]
    for one in scats:
        one.wait_recv()
    for k in range(1, GROUPS):
        line += scat_in[k]
    sub = lax.broadcasted_iota(I32, (8, 128), 0)
    lane8 = lax.broadcasted_iota(I32, (8, 128), 1)
    rows8 = jnp.where((lane8 >> 3) == sub, jnp.broadcast_to(line, (8, 128)), 0.0).astype(BF16)
    l128 = lax.broadcasted_iota(I32, (128, 128), 0)
    m128 = lax.broadcasted_iota(I32, (128, 128), 1)
    fold = jnp.where((l128 & 7) == m128, 1.0, 0.0).astype(BF16)
    result = jnp.dot(rows8, fold, preferred_element_type=F32).astype(BF16)
    coef_ref[...] = result[:PER, :8]

    for one in asks + parts + scats:
        one.wait_send()
    for i in range(ITERS):
        for h in range(len(CHUNKS)):
            for one in flying[i, h]:
                one.wait_send()
    store.wait()


def on_device(rhs, areal_blocks, vertical_blocks, conn_src, conn_count, tile_map, well_cells, well_gain, sens, basis):
    smem = pl.BlockSpec(memory_space=pltpu.SMEM)
    hbm = pl.BlockSpec(memory_space=pl.ANY)
    nc = len(CHUNKS)
    dma = pltpu.SemaphoreType.DMA
    return pl.pallas_call(
        kernel,
        out_shape=(
            jax.ShapeDtypeStruct((1, 2, ROWS, U), BF16),
            jax.ShapeDtypeStruct((PER, MODES // COLUMNS), BF16),
        ),
        in_specs=[smem] * 5 + [hbm] * 5,
        out_specs=(hbm, pl.BlockSpec(memory_space=pltpu.VMEM)),
        scratch_shapes=[
            pltpu.VMEM((ITERS, 3, ROWS, U), BF16),
            pltpu.VMEM((2, NS, U, U), BF16),
            pltpu.VMEM((2, 2, U, U), BF16),
            pltpu.VMEM((2, 3, CELLS), F32),
            pltpu.VMEM((2, CELLS, MODES), BF16),
            pltpu.VMEM((ITERS, NS, ROWS, U), BF16),
            pltpu.VMEM((ITERS, 2, ROWS, U), BF16),
            pltpu.VMEM((NS, 8, 128), I32),
            pltpu.VMEM((NS, 8, 128), I32),
            pltpu.VMEM((COLUMNS, 8, 128), F32),
            pltpu.VMEM((COLUMNS, 8, 128), F32),
            pltpu.VMEM((GROUPS, 1, 128), F32),
            pltpu.VMEM((GROUPS, 1, 128), F32),
            pltpu.VMEM((2, ROWS, U), BF16),
        ]
        + [pltpu.VMEM((NS, rows, U), BF16) for _ in range(ITERS) for _, rows in CHUNKS]
        + [
            dma((5,)),
            dma,
            dma((NS,)),
            dma((NS,)),
            dma((ITERS, nc, NS)),
            dma((ITERS, nc, NS)),
            dma((ITERS, nc, 2)),
            dma((ITERS, nc, 2)),
            dma((COLUMNS,)),
            dma((COLUMNS,)),
            dma((GROUPS,)),
            dma((GROUPS,)),
        ],
        compiler_params=pltpu.CompilerParams(
            collective_id=0, has_side_effects=True, vmem_limit_bytes=56 * 1024 * 1024
        ),
        name="sweeps",
    )(conn_src, conn_count, tile_map, well_cells, well_gain, rhs, areal_blocks, vertical_blocks, sens, basis)


def solution(mesh):
    in_specs = (
        P("areal", "layer", None, None),
        P("areal", "layer", None, None, None),
        P("areal", "layer", None, None, None),
        P("areal", "layer", None),
        P("areal", "layer"),
        P(),
        P("areal", "layer", None),
        P("areal", "layer", None),
        P("areal", "layer", None, None),
        P("areal", "layer", None, None),
    )
    out_specs = (P("areal", "layer", None, None), P("layer", "areal"))
    return jax.shard_map(on_device, mesh=mesh, in_specs=in_specs, out_specs=out_specs, check_vma=False)
```

```python
import jax
import jax.numpy as jnp
from jax import lax
from jax.experimental import pallas as pl
from jax.experimental.pallas import tpu as pltpu
from jax.sharding import PartitionSpec as P

ITERS = 3
COLUMNS = 32
GROUPS = 16
ROWS = 112
U = 384
CELLS = 128
MODES = 256
NS = 6
WELLS = 4
PER = ROWS // GROUPS
OFFSETS = (1, 2, -1, -2, 16, 17)
ORDER = (5, 4, 0, 1, 2, 3)
CHUNKS = ((0, 64), (64, 48))
MESH = pl.DeviceIdType.MESH
F32, BF16, I32 = jnp.float32, jnp.bfloat16, jnp.int32


def kernel(
    conn_src,
    conn_count,
    tile_map,
    well_cells,
    well_gain,
    rhs_hbm,
    areal_hbm,
    vert_hbm,
    sens_hbm,
    basis_hbm,
    adjoint_hbm,
    coef_ref,
    lam,
    w,
    v,
    sens,
    basis,
    send,
    recvz,
    req_out,
    req_in,
    part,
    part_in,
    scat,
    scat_in,
    adj,
    *rest,
):
    recv = [[rest[i * len(CHUNKS) + h] for h in range(len(CHUNKS))] for i in range(ITERS)]
    (
        load_sem,
        out_sem,
        req_ss,
        req_rs,
        a_ss,
        a_rs,
        z_ss,
        z_rs,
        p_ss,
        p_rs,
        s_ss,
        s_rs,
    ) = rest[ITERS * len(CHUNKS) :]
    c, g = lax.axis_index("areal"), lax.axis_index("layer")

    loads = [
        pltpu.make_async_copy(rhs_hbm.at[0], lam.at[0, pl.ds(0, 2)], load_sem.at[0]),
        pltpu.make_async_copy(vert_hbm.at[0], v, load_sem.at[1]),
        pltpu.make_async_copy(areal_hbm.at[0], w, load_sem.at[2]),
        pltpu.make_async_copy(sens_hbm.at[0], sens, load_sem.at[3]),
        pltpu.make_async_copy(basis_hbm.at[0], basis, load_sem.at[4]),
    ]
    for one in loads:
        one.start()

    barrier = pltpu.get_barrier_semaphore()
    for k in range(1, COLUMNS):
        pl.semaphore_signal(barrier, inc=1, device_id=(lax.rem(c + k, COLUMNS), g), device_id_type=MESH)
    for k in range(1, GROUPS):
        pl.semaphore_signal(barrier, inc=1, device_id=(c, lax.rem(g + k, GROUPS)), device_id_type=MESH)

    count = conn_count[0, 0]
    where, wanted = [], []
    for s in range(NS):
        place = tile_map[conn_src[0, 0, s]]
        delta = lax.rem((place >> 1) - c + COLUMNS, COLUMNS)
        at = I32(0)
        for k, offset in enumerate(OFFSETS):
            at = jnp.where(delta == offset % COLUMNS, I32(k), at)
        where.append(at)
        wanted.append(jnp.where(s < count, place & 1, I32(2)))
    for k in range(NS):
        ask = I32(2)
        for s in range(NS):
            ask = jnp.where(where[s] == k, wanted[s], ask)
        req_out[k] = jnp.full((8, 128), ask, I32)
    part[...] = jnp.zeros((COLUMNS, 8, 128), F32)
    for i in range(ITERS):
        lam[i, 2] = jnp.zeros((ROWS, U), BF16)

    pl.semaphore_wait(barrier, COLUMNS + GROUPS - 2)

    asks = []
    for k in ORDER:
        one = pltpu.make_async_remote_copy(
            req_out.at[k], req_in.at[k], req_ss.at[k], req_rs.at[k],
            device_id=(lax.rem(c + OFFSETS[k] + COLUMNS, COLUMNS), g), device_id_type=MESH,
        )
        one.start()
        asks.append(one)

    up, down = lax.rem(g + 1, GROUPS), lax.rem(g + GROUPS - 1, GROUPS)

    def send_vertical(i, h):
        first, rows = CHUNKS[h]
        at = pl.ds(first, rows)
        out = []
        for side, to in ((0, up), (1, down)):
            one = pltpu.make_async_remote_copy(
                lam.at[i, 1 - side, at], recvz.at[i, side, at], z_ss.at[i, h, side], z_rs.at[i, h, side],
                device_id=(c, to), device_id_type=MESH,
            )
            one.start()
            out.append(one)
        return out

    def send_areal(i, h, slots, which=ORDER):
        first, rows = CHUNKS[h]
        at = pl.ds(first, rows)
        out = []
        for k in which:
            send[i, k, at] = lam[i, slots[k], at]
            one = pltpu.make_async_remote_copy(
                send.at[i, k, at], recv[i][h].at[k], a_ss.at[i, h, k], a_rs.at[i, h, k],
                device_id=(lax.rem(c - OFFSETS[k] + COLUMNS, COLUMNS), g), device_id_type=MESH,
            )
            one.start()
            out.append(one)
        return out

    flying = {}
    loads[0].wait()
    for h in range(len(CHUNKS)):
        flying[0, h] = send_vertical(0, h)
    slots = [None] * NS
    for k, one in sorted(zip(ORDER, asks), key=lambda pair: pair[0]):
        one.wait_recv()
        slots[k] = jnp.max(req_in[k])
        for h in range(len(CHUNKS)):
            flying[0, h] = flying[0, h] + send_areal(0, h, slots, (k,))

    for one in loads[1:]:
        one.wait()

    cell = lax.broadcasted_iota(I32, (1, CELLS), 1)
    weight = []
    for d in range(2):
        wells = jnp.zeros((1, CELLS), F32)
        for k in range(WELLS):
            wells += jnp.where(cell == well_cells[0, d, k], well_gain[0, d, k], 0.0)
        weight.append([sens[0, d : d + 1] + wells, sens[1, d : d + 1], sens[2, d : d + 1]])

    stored = []
    for i in range(ITERS):
        for h, (first, rows) in enumerate(CHUNKS):
            at = pl.ds(first, rows)
            for one in flying[i, h]:
                one.wait_recv()
            below = jnp.where(g > 0, recvz[i, 0, at], jnp.zeros((rows, U), BF16))
            above = jnp.where(g < GROUPS - 1, recvz[i, 1, at], jnp.zeros((rows, U), BF16))
            sides = ((below, lam[i, 1, at]), (lam[i, 0, at], above))
            chosen = jnp.concatenate([recv[i][h][where[s]] for s in range(NS)], axis=1)
            grads = []
            for d in range(2):
                off = jnp.dot(chosen, w[d].reshape(NS * U, U), preferred_element_type=F32)
                near = jnp.concatenate(sides[d], axis=1)
                off += jnp.dot(near, v[d].reshape(2 * U, U), preferred_element_type=F32)
                new = (lam[0, d, at].astype(F32) - off).astype(BF16)
                if i < ITERS - 1:
                    lam[i + 1, d, at] = new
                else:
                    adj[d, at] = new
                    newf = new.astype(F32)
                    grad = newf[:, :CELLS] * weight[d][0]
                    for p in range(1, 3):
                        grad += newf[:, p * CELLS : (p + 1) * CELLS] * weight[d][p]
                    grads.append(grad.astype(BF16))
            if i < ITERS - 1:
                flying[i + 1, h] = send_areal(i + 1, h, slots) + send_vertical(i + 1, h)
            else:
                grad = jnp.concatenate(grads, axis=1)
                scat_rows = jnp.dot(grad, basis[...].reshape(2 * CELLS, MODES), preferred_element_type=F32)
                part[:, :, first : first + rows] = scat_rows.T.reshape(COLUMNS, 8, rows)

    store = pltpu.make_async_copy(adj, adjoint_hbm.at[0], out_sem)
    store.start()

    parts = []
    for k in range(1, COLUMNS):
        to = lax.rem(c + k, COLUMNS)
        one = pltpu.make_async_remote_copy(
            part.at[to], part_in.at[k], p_ss.at[k], p_rs.at[k], device_id=(to, g), device_id_type=MESH
        )
        one.start()
        parts.append(one)

    big = lax.broadcasted_iota(I32, (8 * 128, 128), 0)
    lane = lax.broadcasted_iota(I32, (8 * 128, 128), 1)
    row = big & 127
    pick = jnp.where((row < ROWS) & (lane == 8 * lax.rem(row, PER) + (big >> 7)), 1.0, 0.0).astype(BF16)
    group = lax.broadcasted_iota(I32, (GROUPS, 128), 0)
    held = lax.broadcasted_iota(I32, (GROUPS, 128), 1)
    mine = (held >= PER * group) & (held < PER * group + PER)

    total = part[c]
    for one in parts:
        one.wait_recv()
    for k in range(1, COLUMNS):
        total += part_in[k]
    spread = jnp.concatenate(
        [jnp.where(mine, jnp.broadcast_to(total[m : m + 1], (GROUPS, 128)), 0.0).astype(BF16) for m in range(8)],
        axis=1,
    )
    packed = jnp.dot(spread, pick, preferred_element_type=F32)
    scat[...] = packed.reshape(GROUPS, 1, 128)

    scats = []
    for k in range(1, GROUPS):
        to = lax.rem(g + k, GROUPS)
        one = pltpu.make_async_remote_copy(
            scat.at[to], scat_in.at[k], s_ss.at[k], s_rs.at[k], device_id=(c, to), device_id_type=MESH
        )
        one.start()
        scats.append(one)
    line = scat[g]
    for one in scats:
        one.wait_recv()
    for k in range(1, GROUPS):
        line += scat_in[k]
    sub = lax.broadcasted_iota(I32, (8, 128), 0)
    lane8 = lax.broadcasted_iota(I32, (8, 128), 1)
    rows8 = jnp.where((lane8 >> 3) == sub, jnp.broadcast_to(line, (8, 128)), 0.0).astype(BF16)
    l128 = lax.broadcasted_iota(I32, (128, 128), 0)
    m128 = lax.broadcasted_iota(I32, (128, 128), 1)
    fold = jnp.where((l128 & 7) == m128, 1.0, 0.0).astype(BF16)
    result = jnp.dot(rows8, fold, preferred_element_type=F32).astype(BF16)
    coef_ref[...] = result[:PER, :8]

    for one in asks + parts + scats:
        one.wait_send()
    for i in range(ITERS):
        for h in range(len(CHUNKS)):
            for one in flying[i, h]:
                one.wait_send()
    store.wait()


def hand_over(adj, coef, adjoint_ref, coef_ref):
    adjoint_ref[...] = adj[...]
    coef_ref[...] = coef[...]


def on_device(rhs, areal_blocks, vertical_blocks, conn_src, conn_count, tile_map, well_cells, well_gain, sens, basis):
    smem = pl.BlockSpec(memory_space=pltpu.SMEM)
    hbm = pl.BlockSpec(memory_space=pl.ANY)
    nc = len(CHUNKS)
    dma = pltpu.SemaphoreType.DMA
    adj, coef = pl.pallas_call(
        kernel,
        out_shape=(
            jax.ShapeDtypeStruct((1, 2, ROWS, U), BF16),
            jax.ShapeDtypeStruct((PER, MODES // COLUMNS), BF16),
        ),
        in_specs=[smem] * 5 + [hbm] * 5,
        out_specs=(hbm, pl.BlockSpec(memory_space=pltpu.VMEM)),
        scratch_shapes=[
            pltpu.VMEM((ITERS, 3, ROWS, U), BF16),
            pltpu.VMEM((2, NS, U, U), BF16),
            pltpu.VMEM((2, 2, U, U), BF16),
            pltpu.VMEM((3, 2, CELLS), F32),
            pltpu.VMEM((2, CELLS, MODES), BF16),
            pltpu.VMEM((ITERS, NS, ROWS, U), BF16),
            pltpu.VMEM((ITERS, 2, ROWS, U), BF16),
            pltpu.VMEM((NS, 8, 128), I32),
            pltpu.VMEM((NS, 8, 128), I32),
            pltpu.VMEM((COLUMNS, 8, 128), F32),
            pltpu.VMEM((COLUMNS, 8, 128), F32),
            pltpu.VMEM((GROUPS, 1, 128), F32),
            pltpu.VMEM((GROUPS, 1, 128), F32),
            pltpu.VMEM((2, ROWS, U), BF16),
        ]
        + [pltpu.VMEM((NS, rows, U), BF16) for _ in range(ITERS) for _, rows in CHUNKS]
        + [
            dma((5,)),
            dma,
            dma((NS,)),
            dma((NS,)),
            dma((ITERS, nc, NS)),
            dma((ITERS, nc, NS)),
            dma((ITERS, nc, 2)),
            dma((ITERS, nc, 2)),
            dma((COLUMNS,)),
            dma((COLUMNS,)),
            dma((GROUPS,)),
            dma((GROUPS,)),
        ],
        compiler_params=pltpu.CompilerParams(
            collective_id=0, has_side_effects=True, vmem_limit_bytes=56 * 1024 * 1024
        ),
        name="sweeps",
    )(conn_src, conn_count, tile_map, well_cells, well_gain, rhs, areal_blocks, vertical_blocks, jnp.transpose(sens, (0, 2, 1, 3)), basis)
    vmem = pl.BlockSpec(memory_space=pltpu.VMEM)
    return pl.pallas_call(
        hand_over,
        out_shape=(
            jax.ShapeDtypeStruct((1, 2, ROWS, U), BF16),
            jax.ShapeDtypeStruct((PER, MODES // COLUMNS), BF16),
        ),
        in_specs=[vmem, vmem],
        out_specs=(vmem, vmem),
        name="hand_over",
    )(adj, coef)


def solution(mesh):
    in_specs = (
        P("areal", "layer", None, None),
        P("areal", "layer", None, None, None),
        P("areal", "layer", None, None, None),
        P("areal", "layer", None),
        P("areal", "layer"),
        P(),
        P("areal", "layer", None),
        P("areal", "layer", None),
        P("areal", "layer", None, None),
        P("areal", "layer", None, None),
    )
    out_specs = (P("areal", "layer", None, None), P("layer", "areal"))
    return jax.shard_map(on_device, mesh=mesh, in_specs=in_specs, out_specs=out_specs, check_vma=False)
```

```python
import jax
import jax.numpy as jnp
from jax import lax
from jax.experimental import pallas as pl
from jax.experimental.pallas import tpu as pltpu
from jax.sharding import PartitionSpec as P

ITERS = 3
COLUMNS = 32
GROUPS = 16
ROWS = 112
U = 384
CELLS = 128
MODES = 256
NS = 6
WELLS = 4
PER = ROWS // GROUPS
OFFSETS = (1, 2, -1, -2, 16, 17)
ORDER = (5, 4, 0, 1, 2, 3)
CHUNKS = ((0, 64), (64, 48))
MESH = pl.DeviceIdType.MESH
F32, BF16, I32 = jnp.float32, jnp.bfloat16, jnp.int32


def kernel(
    conn_src,
    conn_count,
    tile_map,
    well_cells,
    well_gain,
    rhs_hbm,
    areal_hbm,
    vert_hbm,
    sens_hbm,
    basis_hbm,
    adjoint_hbm,
    coef_ref,
    lam,
    w,
    v,
    sens,
    basis,
    send,
    recvz,
    req_out,
    req_in,
    part,
    part_in,
    scat,
    scat_in,
    adj,
    slot_ref,
    *rest,
):
    recv = [[rest[i * len(CHUNKS) + h] for h in range(len(CHUNKS))] for i in range(ITERS)]
    (
        load_sem,
        out_sem,
        req_ss,
        req_rs,
        a_ss,
        a_rs,
        z_ss,
        z_rs,
        p_ss,
        p_rs,
        s_ss,
        s_rs,
    ) = rest[ITERS * len(CHUNKS) :]
    c, g = lax.axis_index("areal"), lax.axis_index("layer")

    loads = [
        pltpu.make_async_copy(rhs_hbm.at[0], lam.at[0, pl.ds(0, 2)], load_sem.at[0]),
        pltpu.make_async_copy(vert_hbm.at[0], v, load_sem.at[1]),
        pltpu.make_async_copy(areal_hbm.at[0], w, load_sem.at[2]),
        pltpu.make_async_copy(sens_hbm.at[0], sens, load_sem.at[3]),
        pltpu.make_async_copy(basis_hbm.at[0], basis, load_sem.at[4]),
    ]
    for one in loads:
        one.start()

    barrier = pltpu.get_barrier_semaphore()
    for k in range(1, COLUMNS):
        pl.semaphore_signal(barrier, inc=1, device_id=(lax.rem(c + k, COLUMNS), g), device_id_type=MESH)
    for k in range(1, GROUPS):
        pl.semaphore_signal(barrier, inc=1, device_id=(c, lax.rem(g + k, GROUPS)), device_id_type=MESH)

    count = conn_count[0, 0]
    where, wanted = [], []
    for s in range(NS):
        place = tile_map[conn_src[0, 0, s]]
        delta = lax.rem((place >> 1) - c + COLUMNS, COLUMNS)
        at = I32(0)
        for k, offset in enumerate(OFFSETS):
            at = jnp.where(delta == offset % COLUMNS, I32(k), at)
        where.append(at)
        wanted.append(jnp.where(s < count, place & 1, I32(2)))
    for k in range(NS):
        ask = I32(2)
        for s in range(NS):
            ask = jnp.where(where[s] == k, wanted[s], ask)
        req_out[k] = jnp.full((8, 128), ask, I32)
    part[...] = jnp.zeros((COLUMNS, 8, 128), F32)
    for i in range(ITERS):
        lam[i, 2] = jnp.zeros((ROWS, U), BF16)

    pl.semaphore_wait(barrier, COLUMNS + GROUPS - 2)

    asks = []
    for k in ORDER:
        one = pltpu.make_async_remote_copy(
            req_out.at[k], req_in.at[k], req_ss.at[k], req_rs.at[k],
            device_id=(lax.rem(c + OFFSETS[k] + COLUMNS, COLUMNS), g), device_id_type=MESH,
        )
        one.start()
        asks.append(one)

    up, down = lax.rem(g + 1, GROUPS), lax.rem(g + GROUPS - 1, GROUPS)

    def send_vertical(i, h):
        first, rows = CHUNKS[h]
        at = pl.ds(first, rows)
        out = []
        for side, to in ((0, up), (1, down)):
            one = pltpu.make_async_remote_copy(
                lam.at[i, 1 - side, at], recvz.at[i, side, at], z_ss.at[i, h, side], z_rs.at[i, h, side],
                device_id=(c, to), device_id_type=MESH,
            )
            one.start()
            out.append(one)
        return out

    def tile_copy(i, h, k):
        first, rows = CHUNKS[h]
        return pltpu.make_async_remote_copy(
            send.at[i, k, pl.ds(first, rows)], recv[i][h].at[k], a_ss.at[i, h, k], a_rs.at[i, h, k],
            device_id=(lax.rem(c - OFFSETS[k] + COLUMNS, COLUMNS), g), device_id_type=MESH,
        )

    def send_tile(i, h, k, slot):
        first, rows = CHUNKS[h]
        at = pl.ds(first, rows)
        send[i, k, at] = lam[i, slot, at]
        tile_copy(i, h, k).start()

    def send_areal(i, h, slots):
        for k in ORDER:
            send_tile(i, h, k, slots[k])
        return [tile_copy(i, h, k) for k in range(NS)]

    flying = {}
    loads[0].wait()
    for h in range(len(CHUNKS)):
        flying[0, h] = send_vertical(0, h)
    ask_of = dict(zip(ORDER, asks))

    def serve(order):
        for k in order:
            ask_of[k].wait_recv()
            slot = jnp.max(req_in[k])
            slot_ref[k] = slot
            for h in range(len(CHUNKS)):
                send_tile(0, h, k, slot)

    last = lax.rem(c, 8) >= 6
    pl.when(last)(lambda: serve((0, 1, 4, 5, 2, 3)))
    pl.when(jnp.logical_not(last))(lambda: serve((2, 3, 4, 5, 0, 1)))
    slots = [slot_ref[k] for k in range(NS)]
    for h in range(len(CHUNKS)):
        flying[0, h] = flying[0, h] + [tile_copy(0, h, k) for k in range(NS)]

    for one in loads[1:]:
        one.wait()

    cell = lax.broadcasted_iota(I32, (1, CELLS), 1)
    weight = []
    for d in range(2):
        wells = jnp.zeros((1, CELLS), F32)
        for k in range(WELLS):
            wells += jnp.where(cell == well_cells[0, d, k], well_gain[0, d, k], 0.0)
        weight.append([sens[0, d : d + 1] + wells, sens[1, d : d + 1], sens[2, d : d + 1]])

    stored = []
    for i in range(ITERS):
        for h, (first, rows) in enumerate(CHUNKS):
            at = pl.ds(first, rows)
            for one in flying[i, h]:
                one.wait_recv()
            below = jnp.where(g > 0, recvz[i, 0, at], jnp.zeros((rows, U), BF16))
            above = jnp.where(g < GROUPS - 1, recvz[i, 1, at], jnp.zeros((rows, U), BF16))
            sides = ((below, lam[i, 1, at]), (lam[i, 0, at], above))
            chosen = jnp.concatenate([recv[i][h][where[s]] for s in range(NS)], axis=1)
            grads = []
            for d in range(2):
                off = jnp.dot(chosen, w[d].reshape(NS * U, U), preferred_element_type=F32)
                near = jnp.concatenate(sides[d], axis=1)
                off += jnp.dot(near, v[d].reshape(2 * U, U), preferred_element_type=F32)
                new = (lam[0, d, at].astype(F32) - off).astype(BF16)
                if i < ITERS - 1:
                    lam[i + 1, d, at] = new
                else:
                    adj[d, at] = new
                    newf = new.astype(F32)
                    grad = newf[:, :CELLS] * weight[d][0]
                    for p in range(1, 3):
                        grad += newf[:, p * CELLS : (p + 1) * CELLS] * weight[d][p]
                    grads.append(grad.astype(BF16))
            if i < ITERS - 1:
                flying[i + 1, h] = send_areal(i + 1, h, slots) + send_vertical(i + 1, h)
            else:
                grad = jnp.concatenate(grads, axis=1)
                scat_rows = jnp.dot(grad, basis[...].reshape(2 * CELLS, MODES), preferred_element_type=F32)
                part[:, :, first : first + rows] = scat_rows.T.reshape(COLUMNS, 8, rows)

    store = pltpu.make_async_copy(adj, adjoint_hbm.at[0], out_sem)
    store.start()

    parts = []
    for k in range(1, COLUMNS):
        to = lax.rem(c + k, COLUMNS)
        one = pltpu.make_async_remote_copy(
            part.at[to], part_in.at[k], p_ss.at[k], p_rs.at[k], device_id=(to, g), device_id_type=MESH
        )
        one.start()
        parts.append(one)

    big = lax.broadcasted_iota(I32, (8 * 128, 128), 0)
    lane = lax.broadcasted_iota(I32, (8 * 128, 128), 1)
    row = big & 127
    pick = jnp.where((row < ROWS) & (lane == 8 * lax.rem(row, PER) + (big >> 7)), 1.0, 0.0).astype(BF16)
    group = lax.broadcasted_iota(I32, (GROUPS, 128), 0)
    held = lax.broadcasted_iota(I32, (GROUPS, 128), 1)
    mine = (held >= PER * group) & (held < PER * group + PER)

    total = part[c]
    for one in parts:
        one.wait_recv()
    for k in range(1, COLUMNS):
        total += part_in[k]
    spread = jnp.concatenate(
        [jnp.where(mine, jnp.broadcast_to(total[m : m + 1], (GROUPS, 128)), 0.0).astype(BF16) for m in range(8)],
        axis=1,
    )
    packed = jnp.dot(spread, pick, preferred_element_type=F32)
    scat[...] = packed.reshape(GROUPS, 1, 128)

    scats = []
    for k in range(1, GROUPS):
        to = lax.rem(g + k, GROUPS)
        one = pltpu.make_async_remote_copy(
            scat.at[to], scat_in.at[k], s_ss.at[k], s_rs.at[k], device_id=(c, to), device_id_type=MESH
        )
        one.start()
        scats.append(one)
    line = scat[g]
    for one in scats:
        one.wait_recv()
    for k in range(1, GROUPS):
        line += scat_in[k]
    sub = lax.broadcasted_iota(I32, (8, 128), 0)
    lane8 = lax.broadcasted_iota(I32, (8, 128), 1)
    rows8 = jnp.where((lane8 >> 3) == sub, jnp.broadcast_to(line, (8, 128)), 0.0).astype(BF16)
    l128 = lax.broadcasted_iota(I32, (128, 128), 0)
    m128 = lax.broadcasted_iota(I32, (128, 128), 1)
    fold = jnp.where((l128 & 7) == m128, 1.0, 0.0).astype(BF16)
    result = jnp.dot(rows8, fold, preferred_element_type=F32).astype(BF16)
    coef_ref[...] = result[:PER, :8]

    for one in asks + parts + scats:
        one.wait_send()
    for i in range(ITERS):
        for h in range(len(CHUNKS)):
            for one in flying[i, h]:
                one.wait_send()
    store.wait()


def hand_over(adj, coef, adjoint_ref, coef_ref):
    adjoint_ref[...] = adj[...]
    coef_ref[...] = coef[...]


def on_device(rhs, areal_blocks, vertical_blocks, conn_src, conn_count, tile_map, well_cells, well_gain, sens, basis):
    smem = pl.BlockSpec(memory_space=pltpu.SMEM)
    hbm = pl.BlockSpec(memory_space=pl.ANY)
    nc = len(CHUNKS)
    dma = pltpu.SemaphoreType.DMA
    adj, coef = pl.pallas_call(
        kernel,
        out_shape=(
            jax.ShapeDtypeStruct((1, 2, ROWS, U), BF16),
            jax.ShapeDtypeStruct((PER, MODES // COLUMNS), BF16),
        ),
        in_specs=[smem] * 5 + [hbm] * 5,
        out_specs=(hbm, pl.BlockSpec(memory_space=pltpu.VMEM)),
        scratch_shapes=[
            pltpu.VMEM((ITERS, 3, ROWS, U), BF16),
            pltpu.VMEM((2, NS, U, U), BF16),
            pltpu.VMEM((2, 2, U, U), BF16),
            pltpu.VMEM((3, 2, CELLS), F32),
            pltpu.VMEM((2, CELLS, MODES), BF16),
            pltpu.VMEM((ITERS, NS, ROWS, U), BF16),
            pltpu.VMEM((ITERS, 2, ROWS, U), BF16),
            pltpu.VMEM((NS, 8, 128), I32),
            pltpu.VMEM((NS, 8, 128), I32),
            pltpu.VMEM((COLUMNS, 8, 128), F32),
            pltpu.VMEM((COLUMNS, 8, 128), F32),
            pltpu.VMEM((GROUPS, 1, 128), F32),
            pltpu.VMEM((GROUPS, 1, 128), F32),
            pltpu.VMEM((2, ROWS, U), BF16),
            pltpu.SMEM((NS,), I32),
        ]
        + [pltpu.VMEM((NS, rows, U), BF16) for _ in range(ITERS) for _, rows in CHUNKS]
        + [
            dma((5,)),
            dma,
            dma((NS,)),
            dma((NS,)),
            dma((ITERS, nc, NS)),
            dma((ITERS, nc, NS)),
            dma((ITERS, nc, 2)),
            dma((ITERS, nc, 2)),
            dma((COLUMNS,)),
            dma((COLUMNS,)),
            dma((GROUPS,)),
            dma((GROUPS,)),
        ],
        compiler_params=pltpu.CompilerParams(
            collective_id=0, has_side_effects=True, vmem_limit_bytes=56 * 1024 * 1024
        ),
        name="sweeps",
    )(conn_src, conn_count, tile_map, well_cells, well_gain, rhs, areal_blocks, vertical_blocks, jnp.transpose(sens, (0, 2, 1, 3)), basis)
    vmem = pl.BlockSpec(memory_space=pltpu.VMEM)
    return pl.pallas_call(
        hand_over,
        out_shape=(
            jax.ShapeDtypeStruct((1, 2, ROWS, U), BF16),
            jax.ShapeDtypeStruct((PER, MODES // COLUMNS), BF16),
        ),
        in_specs=[vmem, vmem],
        out_specs=(vmem, vmem),
        name="hand_over",
    )(adj, coef)


def solution(mesh):
    in_specs = (
        P("areal", "layer", None, None),
        P("areal", "layer", None, None, None),
        P("areal", "layer", None, None, None),
        P("areal", "layer", None),
        P("areal", "layer"),
        P(),
        P("areal", "layer", None),
        P("areal", "layer", None),
        P("areal", "layer", None, None),
        P("areal", "layer", None, None),
    )
    out_specs = (P("areal", "layer", None, None), P("layer", "areal"))
    return jax.shard_map(on_device, mesh=mesh, in_specs=in_specs, out_specs=out_specs, check_vma=False)
```

```python
import jax
import jax.numpy as jnp
from jax import lax
from jax.experimental import pallas as pl
from jax.experimental.pallas import tpu as pltpu
from jax.sharding import PartitionSpec as P

ITERS = 3
COLUMNS = 32
GROUPS = 16
ROWS = 112
U = 384
CELLS = 128
MODES = 256
NS = 6
WELLS = 4
PER = ROWS // GROUPS
OFFSETS = (1, 2, -1, -2, 16, 17)
ORDER = (5, 4, 0, 1, 2, 3)
CHUNKS = ((0, 64), (64, 48))
MESH = pl.DeviceIdType.MESH
F32, BF16, I32 = jnp.float32, jnp.bfloat16, jnp.int32


def kernel(
    conn_src,
    conn_count,
    tile_map,
    well_cells,
    well_gain,
    rhs_hbm,
    areal_hbm,
    vert_hbm,
    sens_hbm,
    basis_hbm,
    adjoint_hbm,
    coef_ref,
    lam,
    w,
    v,
    sens,
    basis,
    send,
    recvz,
    req_out,
    req_in,
    part,
    part_in,
    scat,
    scat_in,
    adj,
    slot_ref,
    *rest,
):
    recv = [[rest[i * len(CHUNKS) + h] for h in range(len(CHUNKS))] for i in range(ITERS)]
    (
        load_sem,
        out_sem,
        req_ss,
        req_rs,
        a_ss,
        a_rs,
        z_ss,
        z_rs,
        p_ss,
        p_rs,
        s_ss,
        s_rs,
        token,
    ) = rest[ITERS * len(CHUNKS) :]
    c, g = lax.axis_index("areal"), lax.axis_index("layer")

    loads = [
        pltpu.make_async_copy(rhs_hbm.at[0], lam.at[0, pl.ds(0, 2)], load_sem.at[0]),
        pltpu.make_async_copy(vert_hbm.at[0], v, load_sem.at[1]),
        pltpu.make_async_copy(areal_hbm.at[0], w, load_sem.at[2]),
        pltpu.make_async_copy(sens_hbm.at[0], sens, load_sem.at[3]),
        pltpu.make_async_copy(basis_hbm.at[0], basis, load_sem.at[4]),
    ]
    for one in loads:
        one.start()

    barrier = pltpu.get_barrier_semaphore()
    for k in (1, 2, -1, -2, 15, 16, 17):
        pl.semaphore_signal(barrier, inc=1, device_id=(lax.rem(c + k + COLUMNS, COLUMNS), g), device_id_type=MESH)
    for k in (1, GROUPS - 1):
        pl.semaphore_signal(barrier, inc=1, device_id=(c, lax.rem(g + k, GROUPS)), device_id_type=MESH)

    count = conn_count[0, 0]
    where, wanted = [], []
    for s in range(NS):
        place = tile_map[conn_src[0, 0, s]]
        delta = lax.rem((place >> 1) - c + COLUMNS, COLUMNS)
        at = I32(0)
        for k, offset in enumerate(OFFSETS):
            at = jnp.where(delta == offset % COLUMNS, I32(k), at)
        where.append(at)
        wanted.append(jnp.where(s < count, place & 1, I32(2)))
    for k in range(NS):
        ask = I32(2)
        for s in range(NS):
            ask = jnp.where(where[s] == k, wanted[s], ask)
        req_out[k] = jnp.full((8, 128), ask, I32)
    part[...] = jnp.zeros((COLUMNS, 8, 128), F32)
    for i in range(ITERS):
        lam[i, 2] = jnp.zeros((ROWS, U), BF16)

    pl.semaphore_wait(barrier, 9)

    up, down = lax.rem(g + 1, GROUPS), lax.rem(g + GROUPS - 1, GROUPS)

    def tell(n):
        for side, to in ((0, up), (1, down)):
            pl.semaphore_signal(token.at[n, side], inc=1, device_id=(c, to), device_id_type=MESH)

    def hear(n):
        for side in range(2):
            pl.semaphore_wait(token.at[n, side], 1)

    tell(0)
    asks = []
    for k in ORDER:
        one = pltpu.make_async_remote_copy(
            req_out.at[k], req_in.at[k], req_ss.at[k], req_rs.at[k],
            device_id=(lax.rem(c + OFFSETS[k] + COLUMNS, COLUMNS), g), device_id_type=MESH,
        )
        one.start()
        asks.append(one)

    def send_vertical(i, h):
        first, rows = CHUNKS[h]
        at = pl.ds(first, rows)
        out = []
        for side, to in ((0, up), (1, down)):
            one = pltpu.make_async_remote_copy(
                lam.at[i, 1 - side, at], recvz.at[i, side, at], z_ss.at[i, h, side], z_rs.at[i, h, side],
                device_id=(c, to), device_id_type=MESH,
            )
            one.start()
            out.append(one)
        return out

    def tile_copy(i, h, k):
        first, rows = CHUNKS[h]
        return pltpu.make_async_remote_copy(
            send.at[i, k, pl.ds(first, rows)], recv[i][h].at[k], a_ss.at[i, h, k], a_rs.at[i, h, k],
            device_id=(lax.rem(c - OFFSETS[k] + COLUMNS, COLUMNS), g), device_id_type=MESH,
        )

    def send_tile(i, h, k, slot):
        first, rows = CHUNKS[h]
        at = pl.ds(first, rows)
        send[i, k, at] = lam[i, slot, at]
        tile_copy(i, h, k).start()

    def send_areal(i, h, slots):
        for k in ORDER:
            send_tile(i, h, k, slots[k])
        return [tile_copy(i, h, k) for k in range(NS)]

    flying = {}
    loads[0].wait()
    for h in range(len(CHUNKS)):
        flying[0, h] = send_vertical(0, h)
    ask_of = dict(zip(ORDER, asks))

    def serve(order):
        for k in order:
            ask_of[k].wait_recv()
            slot = jnp.max(req_in[k])
            slot_ref[k] = slot
            for h in range(len(CHUNKS)):
                send_tile(0, h, k, slot)

    last = lax.rem(c, 8) >= 6
    pl.when(last)(lambda: serve((0, 1, 4, 5, 2, 3)))
    pl.when(jnp.logical_not(last))(lambda: serve((2, 3, 4, 5, 0, 1)))
    slots = [slot_ref[k] for k in range(NS)]
    for h in range(len(CHUNKS)):
        flying[0, h] = flying[0, h] + [tile_copy(0, h, k) for k in range(NS)]

    for one in loads[1:]:
        one.wait()

    cell = lax.broadcasted_iota(I32, (1, CELLS), 1)
    weight = []
    for d in range(2):
        wells = jnp.zeros((1, CELLS), F32)
        for k in range(WELLS):
            wells += jnp.where(cell == well_cells[0, d, k], well_gain[0, d, k], 0.0)
        weight.append([sens[0, d : d + 1] + wells, sens[1, d : d + 1], sens[2, d : d + 1]])

    stored = []
    for i in range(ITERS):
        for h, (first, rows) in enumerate(CHUNKS):
            at = pl.ds(first, rows)
            step = i * len(CHUNKS) + h
            hear(step)
            tell(step + 1)
            for one in flying[i, h]:
                one.wait_recv()
            below = jnp.where(g > 0, recvz[i, 0, at], jnp.zeros((rows, U), BF16))
            above = jnp.where(g < GROUPS - 1, recvz[i, 1, at], jnp.zeros((rows, U), BF16))
            sides = ((below, lam[i, 1, at]), (lam[i, 0, at], above))
            chosen = jnp.concatenate([recv[i][h][where[s]] for s in range(NS)], axis=1)
            grads = []
            for d in range(2):
                off = jnp.dot(chosen, w[d].reshape(NS * U, U), preferred_element_type=F32)
                near = jnp.concatenate(sides[d], axis=1)
                off += jnp.dot(near, v[d].reshape(2 * U, U), preferred_element_type=F32)
                new = (lam[0, d, at].astype(F32) - off).astype(BF16)
                if i < ITERS - 1:
                    lam[i + 1, d, at] = new
                else:
                    adj[d, at] = new
                    newf = new.astype(F32)
                    grad = newf[:, :CELLS] * weight[d][0]
                    for p in range(1, 3):
                        grad += newf[:, p * CELLS : (p + 1) * CELLS] * weight[d][p]
                    grads.append(grad.astype(BF16))
            if i < ITERS - 1:
                flying[i + 1, h] = send_areal(i + 1, h, slots) + send_vertical(i + 1, h)
            else:
                grad = jnp.concatenate(grads, axis=1)
                scat_rows = jnp.dot(grad, basis[...].reshape(2 * CELLS, MODES), preferred_element_type=F32)
                part[:, :, first : first + rows] = scat_rows.T.reshape(COLUMNS, 8, rows)

    store = pltpu.make_async_copy(adj, adjoint_hbm.at[0], out_sem)
    store.start()

    parts = []
    for k in range(1, COLUMNS):
        to = lax.rem(c + k, COLUMNS)
        one = pltpu.make_async_remote_copy(
            part.at[to], part_in.at[k], p_ss.at[k], p_rs.at[k], device_id=(to, g), device_id_type=MESH
        )
        one.start()
        parts.append(one)

    big = lax.broadcasted_iota(I32, (8 * 128, 128), 0)
    lane = lax.broadcasted_iota(I32, (8 * 128, 128), 1)
    row = big & 127
    pick = jnp.where((row < ROWS) & (lane == 8 * lax.rem(row, PER) + (big >> 7)), 1.0, 0.0).astype(BF16)
    group = lax.broadcasted_iota(I32, (GROUPS, 128), 0)
    held = lax.broadcasted_iota(I32, (GROUPS, 128), 1)
    mine = (held >= PER * group) & (held < PER * group + PER)

    total = part[c]
    for one in parts:
        one.wait_recv()
    for k in range(1, COLUMNS):
        total += part_in[k]
    spread = jnp.concatenate(
        [jnp.where(mine, jnp.broadcast_to(total[m : m + 1], (GROUPS, 128)), 0.0).astype(BF16) for m in range(8)],
        axis=1,
    )
    packed = jnp.dot(spread, pick, preferred_element_type=F32)
    scat[...] = packed.reshape(GROUPS, 1, 128)

    hear(ITERS * len(CHUNKS))
    scats = []
    for k in range(1, GROUPS):
        to = lax.rem(g + k, GROUPS)
        one = pltpu.make_async_remote_copy(
            scat.at[to], scat_in.at[k], s_ss.at[k], s_rs.at[k], device_id=(c, to), device_id_type=MESH
        )
        one.start()
        scats.append(one)
    line = scat[g]
    for one in scats:
        one.wait_recv()
    for k in range(1, GROUPS):
        line += scat_in[k]
    sub = lax.broadcasted_iota(I32, (8, 128), 0)
    lane8 = lax.broadcasted_iota(I32, (8, 128), 1)
    rows8 = jnp.where((lane8 >> 3) == sub, jnp.broadcast_to(line, (8, 128)), 0.0).astype(BF16)
    l128 = lax.broadcasted_iota(I32, (128, 128), 0)
    m128 = lax.broadcasted_iota(I32, (128, 128), 1)
    fold = jnp.where((l128 & 7) == m128, 1.0, 0.0).astype(BF16)
    result = jnp.dot(rows8, fold, preferred_element_type=F32).astype(BF16)
    coef_ref[...] = result[:PER, :8]

    for one in asks + parts + scats:
        one.wait_send()
    for i in range(ITERS):
        for h in range(len(CHUNKS)):
            for one in flying[i, h]:
                one.wait_send()
    store.wait()


def hand_over(adj, coef, adjoint_ref, coef_ref):
    adjoint_ref[...] = adj[...]
    coef_ref[...] = coef[...]


def on_device(rhs, areal_blocks, vertical_blocks, conn_src, conn_count, tile_map, well_cells, well_gain, sens, basis):
    smem = pl.BlockSpec(memory_space=pltpu.SMEM)
    hbm = pl.BlockSpec(memory_space=pl.ANY)
    nc = len(CHUNKS)
    dma = pltpu.SemaphoreType.DMA
    adj, coef = pl.pallas_call(
        kernel,
        out_shape=(
            jax.ShapeDtypeStruct((1, 2, ROWS, U), BF16),
            jax.ShapeDtypeStruct((PER, MODES // COLUMNS), BF16),
        ),
        in_specs=[smem] * 5 + [hbm] * 5,
        out_specs=(hbm, pl.BlockSpec(memory_space=pltpu.VMEM)),
        scratch_shapes=[
            pltpu.VMEM((ITERS, 3, ROWS, U), BF16),
            pltpu.VMEM((2, NS, U, U), BF16),
            pltpu.VMEM((2, 2, U, U), BF16),
            pltpu.VMEM((3, 2, CELLS), F32),
            pltpu.VMEM((2, CELLS, MODES), BF16),
            pltpu.VMEM((ITERS, NS, ROWS, U), BF16),
            pltpu.VMEM((ITERS, 2, ROWS, U), BF16),
            pltpu.VMEM((NS, 8, 128), I32),
            pltpu.VMEM((NS, 8, 128), I32),
            pltpu.VMEM((COLUMNS, 8, 128), F32),
            pltpu.VMEM((COLUMNS, 8, 128), F32),
            pltpu.VMEM((GROUPS, 1, 128), F32),
            pltpu.VMEM((GROUPS, 1, 128), F32),
            pltpu.VMEM((2, ROWS, U), BF16),
            pltpu.SMEM((NS,), I32),
        ]
        + [pltpu.VMEM((NS, rows, U), BF16) for _ in range(ITERS) for _, rows in CHUNKS]
        + [
            dma((5,)),
            dma,
            dma((NS,)),
            dma((NS,)),
            dma((ITERS, nc, NS)),
            dma((ITERS, nc, NS)),
            dma((ITERS, nc, 2)),
            dma((ITERS, nc, 2)),
            dma((COLUMNS,)),
            dma((COLUMNS,)),
            dma((GROUPS,)),
            dma((GROUPS,)),
            pltpu.SemaphoreType.REGULAR((ITERS * nc + 1, 2)),
        ],
        compiler_params=pltpu.CompilerParams(
            collective_id=0, has_side_effects=True, vmem_limit_bytes=56 * 1024 * 1024
        ),
        name="sweeps",
    )(conn_src, conn_count, tile_map, well_cells, well_gain, rhs, areal_blocks, vertical_blocks, jnp.transpose(sens, (0, 2, 1, 3)), basis)
    vmem = pl.BlockSpec(memory_space=pltpu.VMEM)
    return pl.pallas_call(
        hand_over,
        out_shape=(
            jax.ShapeDtypeStruct((1, 2, ROWS, U), BF16),
            jax.ShapeDtypeStruct((PER, MODES // COLUMNS), BF16),
        ),
        in_specs=[vmem, vmem],
        out_specs=(vmem, vmem),
        name="hand_over",
    )(adj, coef)


def solution(mesh):
    in_specs = (
        P("areal", "layer", None, None),
        P("areal", "layer", None, None, None),
        P("areal", "layer", None, None, None),
        P("areal", "layer", None),
        P("areal", "layer"),
        P(),
        P("areal", "layer", None),
        P("areal", "layer", None),
        P("areal", "layer", None, None),
        P("areal", "layer", None, None),
    )
    out_specs = (P("areal", "layer", None, None), P("layer", "areal"))
    return jax.shard_map(on_device, mesh=mesh, in_specs=in_specs, out_specs=out_specs, check_vma=False)
```

```python
import jax
import jax.numpy as jnp
from jax import lax
from jax.experimental import pallas as pl
from jax.experimental.pallas import tpu as pltpu
from jax.sharding import PartitionSpec as P

ITERS = 3
COLUMNS = 32
GROUPS = 16
ROWS = 112
U = 384
CELLS = 128
MODES = 256
NS = 6
WELLS = 4
PER = ROWS // GROUPS
OFFSETS = (1, 2, -1, -2, 16, 17)
ORDER = (5, 4, 0, 1, 2, 3)
CHUNKS = ((0, 64), (64, 48))
MESH = pl.DeviceIdType.MESH
F32, BF16, I32 = jnp.float32, jnp.bfloat16, jnp.int32


def kernel(
    conn_src,
    conn_count,
    tile_map,
    cells_hbm,
    gain_hbm,
    rhs_hbm,
    areal_hbm,
    vert_hbm,
    sens_hbm,
    basis_hbm,
    adjoint_hbm,
    coef_ref,
    lam,
    w,
    v,
    sens,
    basis,
    send,
    recvz,
    req_out,
    req_in,
    part,
    part_in,
    scat,
    scat_in,
    adj,
    slot_ref,
    well_cells,
    well_gain,
    *rest,
):
    recv = [[rest[i * len(CHUNKS) + h] for h in range(len(CHUNKS))] for i in range(ITERS)]
    (
        load_sem,
        out_sem,
        req_ss,
        req_rs,
        a_ss,
        a_rs,
        z_ss,
        z_rs,
        p_ss,
        p_rs,
        s_ss,
        s_rs,
        token,
    ) = rest[ITERS * len(CHUNKS) :]
    c, g = lax.axis_index("areal"), lax.axis_index("layer")

    loads = [
        pltpu.make_async_copy(rhs_hbm.at[0], lam.at[0, pl.ds(0, 2)], load_sem.at[0]),
        pltpu.make_async_copy(vert_hbm.at[0], v, load_sem.at[1]),
        pltpu.make_async_copy(areal_hbm.at[0], w, load_sem.at[2]),
        pltpu.make_async_copy(sens_hbm.at[0], sens, load_sem.at[3]),
        pltpu.make_async_copy(basis_hbm.at[0], basis, load_sem.at[4]),
        pltpu.make_async_copy(cells_hbm, well_cells, load_sem.at[5]),
        pltpu.make_async_copy(gain_hbm, well_gain, load_sem.at[6]),
    ]
    for one in loads:
        one.start()

    barrier = pltpu.get_barrier_semaphore()
    for k in (1, 2, -1, -2, 15, 16, 17):
        pl.semaphore_signal(barrier, inc=1, device_id=(lax.rem(c + k + COLUMNS, COLUMNS), g), device_id_type=MESH)
    for k in (1, GROUPS - 1):
        pl.semaphore_signal(barrier, inc=1, device_id=(c, lax.rem(g + k, GROUPS)), device_id_type=MESH)

    count = conn_count[0, 0]
    where, wanted = [], []
    for s in range(NS):
        place = tile_map[conn_src[0, 0, s]]
        delta = lax.rem((place >> 1) - c + COLUMNS, COLUMNS)
        at = I32(0)
        for k, offset in enumerate(OFFSETS):
            at = jnp.where(delta == offset % COLUMNS, I32(k), at)
        where.append(at)
        wanted.append(jnp.where(s < count, place & 1, I32(2)))
    for k in range(NS):
        ask = I32(2)
        for s in range(NS):
            ask = jnp.where(where[s] == k, wanted[s], ask)
        req_out[k] = jnp.full((8, 128), ask, I32)
    part[...] = jnp.zeros((COLUMNS, 8, 128), F32)
    for i in range(ITERS):
        lam[i, 2] = jnp.zeros((ROWS, U), BF16)

    pl.semaphore_wait(barrier, 9)

    up, down = lax.rem(g + 1, GROUPS), lax.rem(g + GROUPS - 1, GROUPS)

    def tell(n):
        for side, to in ((0, up), (1, down)):
            pl.semaphore_signal(token.at[n, side], inc=1, device_id=(c, to), device_id_type=MESH)

    def hear(n):
        for side in range(2):
            pl.semaphore_wait(token.at[n, side], 1)

    tell(0)
    asks = []
    for k in ORDER:
        one = pltpu.make_async_remote_copy(
            req_out.at[k], req_in.at[k], req_ss.at[k], req_rs.at[k],
            device_id=(lax.rem(c + OFFSETS[k] + COLUMNS, COLUMNS), g), device_id_type=MESH,
        )
        one.start()
        asks.append(one)

    def send_vertical(i, h):
        first, rows = CHUNKS[h]
        at = pl.ds(first, rows)
        out = []
        for side, to in ((0, up), (1, down)):
            one = pltpu.make_async_remote_copy(
                lam.at[i, 1 - side, at], recvz.at[i, side, at], z_ss.at[i, h, side], z_rs.at[i, h, side],
                device_id=(c, to), device_id_type=MESH,
            )
            one.start()
            out.append(one)
        return out

    def tile_copy(i, h, k):
        first, rows = CHUNKS[h]
        return pltpu.make_async_remote_copy(
            send.at[i, k, pl.ds(first, rows)], recv[i][h].at[k], a_ss.at[i, h, k], a_rs.at[i, h, k],
            device_id=(lax.rem(c - OFFSETS[k] + COLUMNS, COLUMNS), g), device_id_type=MESH,
        )

    def send_tile(i, h, k, slot):
        first, rows = CHUNKS[h]
        at = pl.ds(first, rows)
        send[i, k, at] = lam[i, slot, at]
        tile_copy(i, h, k).start()

    def send_areal(i, h, slots):
        for k in ORDER:
            send_tile(i, h, k, slots[k])
        return [tile_copy(i, h, k) for k in range(NS)]

    flying = {}
    loads[0].wait()
    for h in range(len(CHUNKS)):
        flying[0, h] = send_vertical(0, h)
    ask_of = dict(zip(ORDER, asks))

    def serve(order):
        for k in order:
            ask_of[k].wait_recv()
            slot = jnp.max(req_in[k])
            slot_ref[k] = slot
            for h in range(len(CHUNKS)):
                send_tile(0, h, k, slot)

    last = lax.rem(c, 8) >= 6
    pl.when(last)(lambda: serve((0, 1, 4, 5, 2, 3)))
    pl.when(jnp.logical_not(last))(lambda: serve((2, 3, 4, 5, 0, 1)))
    slots = [slot_ref[k] for k in range(NS)]
    for h in range(len(CHUNKS)):
        flying[0, h] = flying[0, h] + [tile_copy(0, h, k) for k in range(NS)]

    for one in loads[1:]:
        one.wait()

    cell = lax.broadcasted_iota(I32, (1, CELLS), 1)
    weight = []
    for d in range(2):
        wells = jnp.zeros((1, CELLS), F32)
        for k in range(WELLS):
            wells += jnp.where(cell == well_cells[0, d, k], well_gain[0, d, k], 0.0)
        weight.append([sens[0, d : d + 1] + wells, sens[1, d : d + 1], sens[2, d : d + 1]])

    stored = []
    for i in range(ITERS):
        for h, (first, rows) in enumerate(CHUNKS):
            at = pl.ds(first, rows)
            step = i * len(CHUNKS) + h
            hear(step)
            tell(step + 1)
            for one in flying[i, h]:
                one.wait_recv()
            below = jnp.where(g > 0, recvz[i, 0, at], jnp.zeros((rows, U), BF16))
            above = jnp.where(g < GROUPS - 1, recvz[i, 1, at], jnp.zeros((rows, U), BF16))
            sides = ((below, lam[i, 1, at]), (lam[i, 0, at], above))
            chosen = jnp.concatenate([recv[i][h][where[s]] for s in range(NS)], axis=1)
            grads = []
            for d in range(2):
                off = jnp.dot(chosen, w[d].reshape(NS * U, U), preferred_element_type=F32)
                near = jnp.concatenate(sides[d], axis=1)
                off += jnp.dot(near, v[d].reshape(2 * U, U), preferred_element_type=F32)
                new = (lam[0, d, at].astype(F32) - off).astype(BF16)
                if i < ITERS - 1:
                    lam[i + 1, d, at] = new
                else:
                    adj[d, at] = new
                    newf = new.astype(F32)
                    grad = newf[:, :CELLS] * weight[d][0]
                    for p in range(1, 3):
                        grad += newf[:, p * CELLS : (p + 1) * CELLS] * weight[d][p]
                    grads.append(grad.astype(BF16))
            if i < ITERS - 1:
                flying[i + 1, h] = send_areal(i + 1, h, slots) + send_vertical(i + 1, h)
            else:
                grad = jnp.concatenate(grads, axis=1)
                scat_rows = jnp.dot(grad, basis[...].reshape(2 * CELLS, MODES), preferred_element_type=F32)
                part[:, :, first : first + rows] = scat_rows.T.reshape(COLUMNS, 8, rows)

    store = pltpu.make_async_copy(adj, adjoint_hbm.at[0], out_sem)
    store.start()

    parts = []
    for k in range(1, COLUMNS):
        to = lax.rem(c + k, COLUMNS)
        one = pltpu.make_async_remote_copy(
            part.at[to], part_in.at[k], p_ss.at[k], p_rs.at[k], device_id=(to, g), device_id_type=MESH
        )
        one.start()
        parts.append(one)

    big = lax.broadcasted_iota(I32, (8 * 128, 128), 0)
    lane = lax.broadcasted_iota(I32, (8 * 128, 128), 1)
    row = big & 127
    pick = jnp.where((row < ROWS) & (lane == 8 * lax.rem(row, PER) + (big >> 7)), 1.0, 0.0).astype(BF16)
    group = lax.broadcasted_iota(I32, (GROUPS, 128), 0)
    held = lax.broadcasted_iota(I32, (GROUPS, 128), 1)
    mine = (held >= PER * group) & (held < PER * group + PER)

    total = part[c]
    for one in parts:
        one.wait_recv()
    for k in range(1, COLUMNS):
        total += part_in[k]
    spread = jnp.concatenate(
        [jnp.where(mine, jnp.broadcast_to(total[m : m + 1], (GROUPS, 128)), 0.0).astype(BF16) for m in range(8)],
        axis=1,
    )
    packed = jnp.dot(spread, pick, preferred_element_type=F32)
    scat[...] = packed.reshape(GROUPS, 1, 128)

    hear(ITERS * len(CHUNKS))
    scats = []
    for k in range(1, GROUPS):
        to = lax.rem(g + k, GROUPS)
        one = pltpu.make_async_remote_copy(
            scat.at[to], scat_in.at[k], s_ss.at[k], s_rs.at[k], device_id=(c, to), device_id_type=MESH
        )
        one.start()
        scats.append(one)
    line = scat[g]
    for one in scats:
        one.wait_recv()
    for k in range(1, GROUPS):
        line += scat_in[k]
    sub = lax.broadcasted_iota(I32, (8, 128), 0)
    lane8 = lax.broadcasted_iota(I32, (8, 128), 1)
    rows8 = jnp.where((lane8 >> 3) == sub, jnp.broadcast_to(line, (8, 128)), 0.0).astype(BF16)
    l128 = lax.broadcasted_iota(I32, (128, 128), 0)
    m128 = lax.broadcasted_iota(I32, (128, 128), 1)
    fold = jnp.where((l128 & 7) == m128, 1.0, 0.0).astype(BF16)
    result = jnp.dot(rows8, fold, preferred_element_type=F32).astype(BF16)
    coef_ref[...] = result[:PER, :8]

    for one in asks + parts + scats:
        one.wait_send()
    for i in range(ITERS):
        for h in range(len(CHUNKS)):
            for one in flying[i, h]:
                one.wait_send()
    store.wait()


def hand_over(adj, coef, adjoint_ref, coef_ref):
    adjoint_ref[...] = adj[...]
    coef_ref[...] = coef[...]


def on_device(rhs, areal_blocks, vertical_blocks, conn_src, conn_count, tile_map, well_cells, well_gain, sens, basis):
    smem = pl.BlockSpec(memory_space=pltpu.SMEM)
    hbm = pl.BlockSpec(memory_space=pl.ANY)
    nc = len(CHUNKS)
    dma = pltpu.SemaphoreType.DMA
    adj, coef = pl.pallas_call(
        kernel,
        out_shape=(
            jax.ShapeDtypeStruct((1, 2, ROWS, U), BF16),
            jax.ShapeDtypeStruct((PER, MODES // COLUMNS), BF16),
        ),
        in_specs=[smem] * 3 + [hbm] * 7,
        out_specs=(hbm, pl.BlockSpec(memory_space=pltpu.VMEM)),
        scratch_shapes=[
            pltpu.VMEM((ITERS, 3, ROWS, U), BF16),
            pltpu.VMEM((2, NS, U, U), BF16),
            pltpu.VMEM((2, 2, U, U), BF16),
            pltpu.VMEM((3, 2, CELLS), F32),
            pltpu.VMEM((2, CELLS, MODES), BF16),
            pltpu.VMEM((ITERS, NS, ROWS, U), BF16),
            pltpu.VMEM((ITERS, 2, ROWS, U), BF16),
            pltpu.VMEM((NS, 8, 128), I32),
            pltpu.VMEM((NS, 8, 128), I32),
            pltpu.VMEM((COLUMNS, 8, 128), F32),
            pltpu.VMEM((COLUMNS, 8, 128), F32),
            pltpu.VMEM((GROUPS, 1, 128), F32),
            pltpu.VMEM((GROUPS, 1, 128), F32),
            pltpu.VMEM((2, ROWS, U), BF16),
            pltpu.SMEM((NS,), I32),
            pltpu.SMEM((1, 2, WELLS), I32),
            pltpu.SMEM((1, 2, WELLS), F32),
        ]
        + [pltpu.VMEM((NS, rows, U), BF16) for _ in range(ITERS) for _, rows in CHUNKS]
        + [
            dma((7,)),
            dma,
            dma((NS,)),
            dma((NS,)),
            dma((ITERS, nc, NS)),
            dma((ITERS, nc, NS)),
            dma((ITERS, nc, 2)),
            dma((ITERS, nc, 2)),
            dma((COLUMNS,)),
            dma((COLUMNS,)),
            dma((GROUPS,)),
            dma((GROUPS,)),
            pltpu.SemaphoreType.REGULAR((ITERS * nc + 1, 2)),
        ],
        compiler_params=pltpu.CompilerParams(
            collective_id=0, has_side_effects=True, vmem_limit_bytes=56 * 1024 * 1024
        ),
        name="sweeps",
    )(conn_src, conn_count, tile_map, well_cells, well_gain, rhs, areal_blocks, vertical_blocks, jnp.transpose(sens, (0, 2, 1, 3)), basis)
    vmem = pl.BlockSpec(memory_space=pltpu.VMEM)
    return pl.pallas_call(
        hand_over,
        out_shape=(
            jax.ShapeDtypeStruct((1, 2, ROWS, U), BF16),
            jax.ShapeDtypeStruct((PER, MODES // COLUMNS), BF16),
        ),
        in_specs=[vmem, vmem],
        out_specs=(vmem, vmem),
        name="hand_over",
    )(adj, coef)


def solution(mesh):
    in_specs = (
        P("areal", "layer", None, None),
        P("areal", "layer", None, None, None),
        P("areal", "layer", None, None, None),
        P("areal", "layer", None),
        P("areal", "layer"),
        P(),
        P("areal", "layer", None),
        P("areal", "layer", None),
        P("areal", "layer", None, None),
        P("areal", "layer", None, None),
    )
    out_specs = (P("areal", "layer", None, None), P("layer", "areal"))
    return jax.shard_map(on_device, mesh=mesh, in_specs=in_specs, out_specs=out_specs, check_vma=False)
```
